1024 devices in a mesh: dp: 8 (over z), row: 8 (over x), col: 16 (over y, core).
Axes of the slice: x: 8, y: 8, z: 8, core: 2. Of those that a mesh axis runs over, the one named last changes fastest.
Arguments:
- grad: bfloat16 [8, 4096, 14336], P('dp', 'row', 'col'), may hold values from -6 to 6
- error: bfloat16 [8, 4096, 14336], P('dp', 'row', 'col'), may hold values from -6 to 6
- q_init: float32 [14336, 128], P('col'), may hold values from -6 to 6
Outputs:
- new_error: bfloat16 [8, 4096, 14336], P('dp', 'row', 'col')
- q_factor: float32 [14336, 128], P('col')
The draws below stay inside these ranges and needn't reach their ends.
All inputs are finite; a program needn't handle non-finite values.
Results may differ from the reference program's by a relative error of at most 0.001.
Values sent between devices are 32-bit elements; how exact they have to be, the bound alone decides.
No kernel may reach another device: no remote copies, remote signals or barrier semaphores. Data moves between devices by JAX's collectives and lax.ppermute only.
A program may use at most 32 MiB of HBM per device.

```python
import jax
import jax.numpy as jnp
from jax import lax

ROWS = 4096
COLS = 14336
RANK = 128
ITERS = 2
N_DP = 8


def block_scale(key, shape, cuts, smallest, largest):
    gain = 1.0
    for position, shards_of in cuts:
        heights = jax.random.uniform(jax.random.fold_in(jax.random.fold_in(key, 6), position), (shards_of,), jnp.float32, smallest / len(cuts), largest / len(cuts))
        gain = gain * jnp.repeat(jnp.exp(heights), shape[position] // shards_of).reshape((-1,) + (1,) * (len(shape) - 1 - position))
    return gain


def gaussian(key, dims, width, bound, shards=(), kind=jnp.bfloat16):
    level = block_scale(key, dims, shards, -0.22, 0.18) if shards else 1.0
    array = jax.random.normal(key, dims, jnp.float32) * width * level
    return jnp.minimum(jnp.maximum(array, -bound), bound).astype(kind)


def setup_inputs(seed: int = 0) -> dict:
    keys = jax.random.split(jax.random.key(seed), 4)
    grad = gaussian(keys[0], (N_DP, ROWS, COLS), 1.0, 6.0, ((0, 8), (1, 8), (2, 16)))
    error = gaussian(keys[1], (N_DP, ROWS, COLS), 0.5, 6.0, ((0, 8), (1, 8), (2, 16)))
    q_init = gaussian(keys[2], (COLS, RANK), 1.0, 6.0, ((0, 16),), jnp.float32)
    return dict(grad=grad, error=error, q_init=q_init)


def orthonormal(p_mat):
    gram = jnp.dot(p_mat.T.astype(jnp.float32), p_mat.astype(jnp.float32), precision=lax.Precision.HIGHEST, preferred_element_type=jnp.float32)
    lower = jnp.linalg.cholesky(gram)
    return jax.scipy.linalg.solve_triangular(lower, p_mat.T, lower=True).T

def reference(grad, error, q_init):
    workers = grad.shape[0]
    q_mat = q_init
    p_hat = None
    for step in range(ITERS):
        p_mat = jnp.zeros((grad.shape[1], q_mat.shape[1]), jnp.float32)
        for worker in range(workers):
            comp = grad[worker].astype(jnp.float32) + error[worker].astype(jnp.float32)
            p_mat = p_mat + jnp.dot(comp.astype(jnp.float32), q_mat.astype(jnp.float32), precision=lax.Precision.HIGHEST, preferred_element_type=jnp.float32)
        p_hat = orthonormal(p_mat * (1.0 / workers))
        q_next = jnp.zeros(q_mat.shape, jnp.float32)
        for worker in range(workers):
            comp = grad[worker].astype(jnp.float32) + error[worker].astype(jnp.float32)
            q_next = q_next + jnp.dot(comp.T.astype(jnp.float32), p_hat.astype(jnp.float32), precision=lax.Precision.HIGHEST, preferred_element_type=jnp.float32)
        q_mat = q_next * (1.0 / workers)
    approx = jnp.dot(p_hat.astype(jnp.float32), q_mat.T.astype(jnp.float32), precision=lax.Precision.HIGHEST, preferred_element_type=jnp.float32)
    comp_all = grad.astype(jnp.float32) + error.astype(jnp.float32)
    new_error = (comp_all - approx[None]).astype(jnp.bfloat16)
    return (new_error, q_mat)
```

```python
import jax
import jax.numpy as jnp
from jax import lax
from jax.sharding import PartitionSpec as P

ITERS = 2
HIGHEST = lax.Precision.HIGHEST


def scatter_sum(x, axes):
    count = lax.axis_size(axes)
    pieces = x.reshape(count, x.shape[0] // count, x.shape[1])
    return lax.all_to_all(pieces, axes, 0, 0, tiled=True).sum(axis=0)


def gather_all(piece, axes):
    count = lax.axis_size(axes)
    copies = jnp.broadcast_to(piece[None], (count, *piece.shape))
    return lax.all_to_all(copies, axes, 0, 0, tiled=True).reshape(-1, piece.shape[1])


def total(x, axes):
    return gather_all(scatter_sum(x, axes), axes)


def dot(a, b, contract):
    return lax.dot_general(
        a, b, (contract, ((), ())), precision=HIGHEST, preferred_element_type=jnp.float32
    )


def over_lower(lower, x):
    return jax.scipy.linalg.solve_triangular(lower, x.T, lower=True).T


def shards(grad, error, q_init):
    comp = grad[0].astype(jnp.float32) + error[0].astype(jnp.float32)
    scale = 1.0 / lax.axis_size("dp")
    cols = comp.shape[1]
    q_mat = q_init
    for step in range(ITERS):
        p_mat = total(dot(comp, q_mat, ((1,), (0,))), ("dp", "col")) * scale
        term = dot(comp, p_mat, ((0,), (0,)))
        gram = dot(p_mat, p_mat, ((0,), (0,)))
        both = total(jnp.concatenate([term, gram]) * scale, ("dp", "row"))
        lower = jnp.linalg.cholesky(both[cols:])
        q_mat = over_lower(lower, both[:cols])
    p_hat = over_lower(lower, p_mat)
    approx = dot(p_hat, q_mat, ((1,), (1,)))
    new_error = (comp - approx).astype(jnp.bfloat16)[None]
    return (new_error, q_mat)


def solution(mesh):
    in_specs = (P("dp", "row", "col"), P("dp", "row", "col"), P("col", None))
    out_specs = (P("dp", "row", "col"), P("col", None))
    return jax.shard_map(shards, mesh=mesh, in_specs=in_specs, out_specs=out_specs, check_vma=False)
```

```python
import functools

import jax
import jax.numpy as jnp
from jax import lax
from jax.experimental import pallas as pl
from jax.experimental.pallas import tpu as pltpu
from jax.sharding import Mesh
from jax.sharding import PartitionSpec as P

HIGHEST = lax.Precision.HIGHEST
BLOCK = 32
VMEM_LIMIT = 24 * 2**20


def mm(a, b, on_a, on_b):
    return lax.dot_general(
        a,
        b,
        (((on_a,), (on_b,)), ((), ())),
        precision=HIGHEST,
        preferred_element_type=jnp.float32,
    )


def mm16(a, b):
    return jnp.dot(a, b, preferred_element_type=jnp.float32)


def three_parts(x):
    first = x.astype(jnp.bfloat16)
    rest = x - first.astype(jnp.float32)
    second = rest.astype(jnp.bfloat16)
    third = (rest - second.astype(jnp.float32)).astype(jnp.bfloat16)
    return first, second, third


def add_parts(x, axis):
    n = x.shape[axis] // 3
    a, b, c = (lax.slice_in_dim(x, i * n, (i + 1) * n, axis=axis) for i in range(3))
    return a + (b + c)


def diagonal(gram, axis):
    n = gram.shape[0]
    row = lax.broadcasted_iota(jnp.int32, (n, n), 0)
    lane = lax.broadcasted_iota(jnp.int32, (n, n), 1)
    return jnp.sum(jnp.where(row == lane, gram, 0.0), axis=axis, keepdims=True)


def small_inverse(block, width):
    n = block.shape[0]
    row = lax.broadcasted_iota(jnp.int32, (n, width), 0)
    lane = lax.broadcasted_iota(jnp.int32, (n, width), 1)
    inv = jnp.where(row == lane, 1.0, 0.0)
    cols = [jnp.broadcast_to(block[:, k : k + 1], (n, width)) for k in range(n)]
    for k in range(n):
        scale = lax.rsqrt(cols[k][k : k + 1, :])
        lower = cols[k] * scale
        pivot = inv[k : k + 1, :] * scale
        inv = jnp.where(
            row > k,
            inv - lower * pivot,
            jnp.where(row == k, jnp.broadcast_to(pivot, (n, width)), inv),
        )
        for j in range(k + 1, n):
            low = (j // 8) * 8
            new = cols[j][low:, :] - lower[low:, :] * lower[j : j + 1, :]
            cols[j] = new if low == 0 else jnp.concatenate([cols[j][:low, :], new], axis=0)
    return inv


def lower_inverse(gram):
    n = gram.shape[0]
    row = lax.broadcasted_iota(jnp.int32, (n, n), 0)
    lane = lax.broadcasted_iota(jnp.int32, (n, n), 1)
    left, right = gram, jnp.where(row == lane, 1.0, 0.0)
    out = []
    for start in range(0, n, BLOCK):
        small = small_inverse(left[:BLOCK, start : start + BLOCK], n)[:, :BLOCK]
        new_right = mm(small, right[:BLOCK, :], 1, 0)
        out.append(new_right)
        if start + BLOCK < n:
            new_left = mm(small, left[:BLOCK, :], 1, 0)
            below = new_left[:, start + BLOCK :]
            left = left[BLOCK:, :] - mm(below, new_left, 0, 0)
            right = right[BLOCK:, :] - mm(below, new_right, 0, 0)
    return jnp.concatenate(out, axis=0)


def left_product(grad, error, q_mat, scale):
    parts = jnp.concatenate(three_parts(q_mat), axis=1)
    return add_parts(mm16(grad, parts) + mm16(error, parts), 1) * scale


def first_left_kernel(scale, grad, error, q_mat, out):
    out[...] = left_product(grad[0], error[0], q_mat[...], scale)


def next_left_kernel(scale, grad, error, both, out):
    cols = grad.shape[2]
    both = both[...].reshape(-1, both.shape[2])
    q_mat = both[:cols] * lax.rsqrt(diagonal(both[cols:], 0))
    out[...] = left_product(grad[0], error[0], q_mat, scale)


def right_kernel(scale, grad, error, p_mat, out):
    p_mat = p_mat[...].reshape(-1, p_mat.shape[2])
    p_t = p_mat.T
    parts = jnp.concatenate(three_parts(p_t), axis=0)
    term = add_parts(mm16(parts, grad[0]) + mm16(parts, error[0]), 0).T
    gram = mm(p_t, p_mat, 1, 0)
    both = jnp.concatenate([term, gram], axis=0) * scale
    out[...] = both.reshape(out.shape)


def sum_kernel(pieces, out):
    out[...] = jnp.broadcast_to(jnp.sum(pieces[...], axis=0)[None], out.shape)


def sum_scale_kernel(pieces, inverse, out):
    piece = mm(jnp.sum(pieces[...], axis=0), inverse[...], 1, 1)
    out[...] = jnp.broadcast_to(piece[None], out.shape)


def inverse_kernel(both, out):
    n = out.shape[0]
    gram = both[...].reshape(-1, n)[-n:]
    by_row = lax.rsqrt(diagonal(gram, 1))
    by_lane = lax.rsqrt(diagonal(gram, 0))
    out[...] = lower_inverse(gram * by_row * by_lane)


def last_kernel(grad, error, p_mat, both, new_error, q_factor):
    cols = grad.shape[2]
    p_mat = p_mat[...].reshape(-1, p_mat.shape[2])
    both = both[...].reshape(-1, both.shape[2])
    inverse = lower_inverse(both[cols:])
    q_mat = mm(both[:cols], inverse, 1, 1)
    q_factor[...] = q_mat
    p_hat = mm(p_mat, inverse, 1, 1)
    approx = mm(p_hat, q_mat, 1, 1)
    comp = grad[0].astype(jnp.float32) + error[0].astype(jnp.float32)
    new_error[0] = (comp - approx).astype(jnp.bfloat16)


def call(kernel, shapes, *operands, flops=10**8):
    n_bytes = sum(x.size * x.dtype.itemsize for x in operands)
    single = not isinstance(shapes, tuple)
    outs = (shapes,) if single else shapes
    result = pl.pallas_call(
        kernel,
        out_shape=shapes,
        in_specs=[pl.BlockSpec(memory_space=pltpu.VMEM)] * len(operands),
        out_specs=jax.tree.map(lambda _: pl.BlockSpec(memory_space=pltpu.VMEM), shapes),
        compiler_params=pltpu.CompilerParams(vmem_limit_bytes=VMEM_LIMIT),
        cost_estimate=pl.CostEstimate(
            flops=flops, bytes_accessed=n_bytes + sum(s.size * 4 for s in outs), transcendentals=0
        ),
    )(*operands)
    return result


def f32(*shape):
    return jax.ShapeDtypeStruct(shape, jnp.float32)


def exchange(x, axes):
    return lax.all_to_all(x, axes, 0, 0, tiled=True)


def shards(grad, error, q_init):
    rows, cols = grad.shape[1:]
    rank = q_init.shape[1]
    scale = 1.0 / lax.axis_size("dp")
    left_axes, right_axes = ("dp", "y"), ("dp", "row")
    n_left, n_right = lax.axis_size(left_axes), lax.axis_size(right_axes)
    left_shape = f32(n_left, rows // n_left, rank)
    right_shape = f32(n_right, (cols + rank) // n_right, rank)

    def left_pieces(partial):
        chip = lax.all_gather(partial, "core").sum(axis=0)
        return exchange(chip.reshape(left_shape.shape), left_axes)

    def right_total(p_all):
        partial = call(functools.partial(right_kernel, scale), right_shape, grad, error, p_all)
        pieces = exchange(partial, right_axes)
        return exchange(call(sum_kernel, right_shape, pieces), right_axes)

    partial = call(
        functools.partial(first_left_kernel, scale), f32(rows, rank), grad, error, q_init
    )
    pieces = left_pieces(partial)
    p_all = exchange(call(sum_kernel, left_shape, pieces), left_axes)
    both = right_total(p_all)
    partial = call(functools.partial(next_left_kernel, scale), f32(rows, rank), grad, error, both)
    inverse = call(inverse_kernel, f32(rank, rank), both, flops=4 * 10**9)
    pieces = left_pieces(partial)
    p_all = exchange(call(sum_scale_kernel, left_shape, pieces, inverse), left_axes)
    both = right_total(p_all)
    return call(
        last_kernel,
        (jax.ShapeDtypeStruct(grad.shape, jnp.bfloat16), f32(cols, rank)),
        grad,
        error,
        p_all,
        both,
    )


def solution(mesh):
    size = mesh.devices.shape
    fine = Mesh(mesh.devices.reshape(*size[:2], size[2] // 2, 2), ("dp", "row", "y", "core"))
    block = P("dp", "row", ("y", "core"))
    right = P(("y", "core"), None)
    return jax.shard_map(
        shards, mesh=fine, in_specs=(block, block, right), out_specs=(block, right), check_vma=False
    )
```

```python
import functools

import jax
import jax.numpy as jnp
from jax import lax
from jax.experimental import pallas as pl
from jax.experimental.pallas import tpu as pltpu
from jax.sharding import Mesh
from jax.sharding import PartitionSpec as P

HIGHEST = lax.Precision.HIGHEST
BLOCK = 32
CHUNKS = 4
VMEM_LIMIT = 24 * 2**20
VMEM_MOST = 64 * 2**20 - 400 * 2**10
VMEM = pl.BlockSpec(memory_space=pltpu.VMEM)
HBM = pl.BlockSpec(memory_space=pltpu.HBM)


def mm(a, b, on_a, on_b):
    return lax.dot_general(
        a,
        b,
        (((on_a,), (on_b,)), ((), ())),
        precision=HIGHEST,
        preferred_element_type=jnp.float32,
    )


def mm16(a, b):
    return jnp.dot(a, b, preferred_element_type=jnp.float32)


def three_parts(x):
    first = x.astype(jnp.bfloat16)
    rest = x - first.astype(jnp.float32)
    second = rest.astype(jnp.bfloat16)
    third = (rest - second.astype(jnp.float32)).astype(jnp.bfloat16)
    return first, second, third


def mm_wide(a, b):
    a, b = three_parts(a), three_parts(b)
    wide_a = jnp.concatenate([a[i] for i in (0, 0, 1, 0, 2, 1)], axis=1)
    wide_b = jnp.concatenate([b[i] for i in (0, 1, 0, 2, 0, 1)], axis=1)
    return lax.dot_general(
        wide_a, wide_b, (((1,), (1,)), ((), ())), preferred_element_type=jnp.float32
    )


def add_parts(x, axis):
    n = x.shape[axis] // 3
    a, b, c = (lax.slice_in_dim(x, i * n, (i + 1) * n, axis=axis) for i in range(3))
    return a + (b + c)


def diagonal(gram, axis):
    n = gram.shape[0]
    row = lax.broadcasted_iota(jnp.int32, (n, n), 0)
    lane = lax.broadcasted_iota(jnp.int32, (n, n), 1)
    return jnp.sum(jnp.where(row == lane, gram, 0.0), axis=axis, keepdims=True)


def small_inverse(block, width):
    n = block.shape[0]
    row = lax.broadcasted_iota(jnp.int32, (n, width), 0)
    lane = lax.broadcasted_iota(jnp.int32, (n, width), 1)
    inv = jnp.where(row == lane, 1.0, 0.0)
    cols = [jnp.broadcast_to(block[:, k : k + 1], (n, width)) for k in range(n)]
    for k in range(n):
        scale = lax.rsqrt(cols[k][k : k + 1, :])
        lower = cols[k] * scale
        pivot = inv[k : k + 1, :] * scale
        inv = jnp.where(
            row > k,
            inv - lower * pivot,
            jnp.where(row == k, jnp.broadcast_to(pivot, (n, width)), inv),
        )
        for j in range(k + 1, n):
            low = (j // 8) * 8
            new = cols[j][low:, :] - lower[low:, :] * lower[j : j + 1, :]
            cols[j] = new if low == 0 else jnp.concatenate([cols[j][:low, :], new], axis=0)
    return inv


def lower_inverse(gram):
    n = gram.shape[0]
    row = lax.broadcasted_iota(jnp.int32, (n, n), 0)
    lane = lax.broadcasted_iota(jnp.int32, (n, n), 1)
    left, right = gram, jnp.where(row == lane, 1.0, 0.0)
    out = []
    for start in range(0, n, BLOCK):
        small = small_inverse(left[:BLOCK, start : start + BLOCK], n)[:, :BLOCK]
        new_right = mm(small, right[:BLOCK, :], 1, 0)
        out.append(new_right)
        if start + BLOCK < n:
            new_left = mm(small, left[:BLOCK, :], 1, 0)
            below = new_left[:, start + BLOCK :]
            left = left[BLOCK:, :] - mm(below, new_left, 0, 0)
            right = right[BLOCK:, :] - mm(below, new_right, 0, 0)
    return jnp.concatenate(out, axis=0)


def left_product(grad, error, q_mat, scale):
    parts = jnp.concatenate(three_parts(q_mat), axis=1)
    return add_parts(mm16(grad, parts) + mm16(error, parts), 1) * scale


def first_left_kernel(scale, grad, error, q_mat, out, held, q_held, sems, q_sem):
    rows = held.shape[2]
    q_copy = pltpu.make_async_copy(q_mat, q_held, q_sem)
    q_copy.start()
    copies = []
    for i in range(CHUNKS):
        for k, source in enumerate((grad, error)):
            chunk = source.at[0, pl.ds(i * rows, rows), :]
            copies.append(pltpu.make_async_copy(chunk, held.at[i, k], sems.at[i, k]))
            copies[-1].start()
    q_copy.wait()
    parts = jnp.concatenate(three_parts(q_held[...]), axis=1)
    for i in range(CHUNKS):
        copies[2 * i].wait()
        copies[2 * i + 1].wait()
        product = mm16(held[i].reshape(2 * rows, -1), parts)
        out[pl.ds(i * rows, rows), :] = add_parts(product[:rows] + product[rows:], 1) * scale


def next_left_kernel(scale, grad, error, both, out):
    cols = grad.shape[2]
    both = both[...].reshape(-1, both.shape[2])
    q_mat = both[:cols] * lax.rsqrt(diagonal(both[cols:], 0))
    out[...] = left_product(grad[0], error[0], q_mat, scale)


def right_kernel(scale, grad, error, p_mat, out):
    p_mat = p_mat[...]
    p_t = p_mat.T
    parts = jnp.concatenate(three_parts(p_t), axis=0)
    term = add_parts(mm16(parts, grad[0]) + mm16(parts, error[0]), 0).T
    gram = mm(p_t, p_mat, 1, 0)
    both = jnp.concatenate([term, gram], axis=0) * scale
    out[...] = both.reshape(out.shape)


def sum_kernel(pieces, out):
    out[...] = jnp.broadcast_to(jnp.sum(pieces[...], axis=0)[None], out.shape)


def sum_scale_kernel(pieces, inverse, out):
    piece = mm(jnp.sum(pieces[...], axis=0), inverse[...], 1, 1)
    out[...] = jnp.broadcast_to(piece[None], out.shape)


def inverse_kernel(both, out):
    n = out.shape[0]
    gram = both[...].reshape(-1, n)[-n:]
    by_row = lax.rsqrt(diagonal(gram, 1))
    by_lane = lax.rsqrt(diagonal(gram, 0))
    out[...] = lower_inverse(gram * by_row * by_lane)


def core_half_kernel(partials, out):
    rows = out.shape[0]
    start = pl.multiple_of(lax.axis_index("core") * rows, rows)
    out[...] = partials[0, pl.ds(start, rows), :] + partials[1, pl.ds(start, rows), :]


def last_kernel(grad, error, p_mat, both, new_error, q_factor, held, q_held, sems, q_sem):
    cols = grad.shape[2]
    both = both[...].reshape(-1, both.shape[2])
    inverse = lower_inverse(both[cols:])
    q_mat = mm_wide(both[:cols], inverse)
    q_held[...] = q_mat
    copies = [pltpu.make_async_copy(q_held, q_factor, q_sem)]
    copies[0].start()
    p_hat = mm_wide(p_mat[...], inverse)
    rows = held.shape[1] // CHUNKS
    for i in range(CHUNKS):
        part = pl.ds(i * rows, rows)
        comp = grad[0, part, :].astype(jnp.float32) + error[0, part, :].astype(jnp.float32)
        approx = mm_wide(p_hat[i * rows : (i + 1) * rows], q_mat)
        held[0, part, :] = (comp - approx).astype(jnp.bfloat16)
        chunk = new_error.at[0, part, :]
        copies.append(pltpu.make_async_copy(held.at[0, part, :], chunk, sems.at[i]))
        copies[-1].start()
    for copy in copies:
        copy.wait()


def call(kernel, shapes, *operands, flops=10**8, **more):
    n_bytes = sum(x.size * x.dtype.itemsize for x in operands)
    n_bytes += sum(s.size * s.dtype.itemsize for s in jax.tree.leaves(shapes))
    return pl.pallas_call(
        kernel,
        out_shape=shapes,
        in_specs=more.pop("in_specs", [VMEM] * len(operands)),
        out_specs=more.pop("out_specs", VMEM),
        compiler_params=pltpu.CompilerParams(
            vmem_limit_bytes=more.pop("vmem_limit_bytes", VMEM_LIMIT)
        ),
        cost_estimate=pl.CostEstimate(flops=flops, bytes_accessed=n_bytes, transcendentals=0),
        **more,
    )(*operands)


def f32(*shape):
    return jax.ShapeDtypeStruct(shape, jnp.float32)


def exchange(x, axes):
    return lax.all_to_all(x, axes, 0, 0, tiled=True)


def shards(grad, error, q_init):
    rows, cols = grad.shape[1:]
    rank = q_init.shape[1]
    scale = 1.0 / lax.axis_size("dp")
    left_axes, right_axes = ("dp", "y"), ("dp", "row")
    n_left, n_right = lax.axis_size(left_axes), lax.axis_size(right_axes)
    half = rows // lax.axis_size("core")
    left_shape = f32(n_left, half // n_left, rank)
    right_shape = f32(n_right, (cols + rank) // n_right, rank)
    chunk = rows // CHUNKS

    def left_pieces(partial):
        chip = call(core_half_kernel, f32(half, rank), lax.all_gather(partial, "core"))
        return exchange(chip.reshape(left_shape.shape), left_axes)

    def left_gathered(pieces):
        mine = exchange(pieces, left_axes).reshape(half, rank)
        return lax.all_gather(mine, "core", tiled=True)

    def right_total(p_all):
        partial = call(functools.partial(right_kernel, scale), right_shape, grad, error, p_all)
        pieces = exchange(partial, right_axes)
        return exchange(call(sum_kernel, right_shape, pieces), right_axes)

    partial = call(
        functools.partial(first_left_kernel, scale),
        f32(rows, rank),
        grad,
        error,
        q_init,
        in_specs=[HBM] * 3,
        vmem_limit_bytes=VMEM_MOST,
        scratch_shapes=[
            pltpu.VMEM((CHUNKS, 2, chunk, cols), jnp.bfloat16),
            pltpu.VMEM((cols, rank), jnp.float32),
            pltpu.SemaphoreType.DMA((CHUNKS, 2)),
            pltpu.SemaphoreType.DMA,
        ],
    )
    pieces = left_pieces(partial)
    p_all = left_gathered(call(sum_kernel, left_shape, pieces))
    both = right_total(p_all)
    partial = call(functools.partial(next_left_kernel, scale), f32(rows, rank), grad, error, both)
    inverse = call(inverse_kernel, f32(rank, rank), both, flops=4 * 10**9)
    pieces = left_pieces(partial)
    p_all = left_gathered(call(sum_scale_kernel, left_shape, pieces, inverse))
    both = right_total(p_all)
    return call(
        last_kernel,
        (jax.ShapeDtypeStruct(grad.shape, jnp.bfloat16), f32(cols, rank)),
        grad,
        error,
        p_all,
        both,
        out_specs=(HBM, HBM),
        scratch_shapes=[
            pltpu.VMEM((1, rows, cols), jnp.bfloat16),
            pltpu.VMEM((cols, rank), jnp.float32),
            pltpu.SemaphoreType.DMA((CHUNKS,)),
            pltpu.SemaphoreType.DMA,
        ],
    )


def solution(mesh):
    size = mesh.devices.shape
    fine = Mesh(mesh.devices.reshape(*size[:2], size[2] // 2, 2), ("dp", "row", "y", "core"))
    block = P("dp", "row", ("y", "core"))
    right = P(("y", "core"), None)
    return jax.shard_map(
        shards, mesh=fine, in_specs=(block, block, right), out_specs=(block, right), check_vma=False
    )
```

```python
import functools

import jax
import jax.numpy as jnp
from jax import lax
from jax.experimental import pallas as pl
from jax.experimental.pallas import tpu as pltpu
from jax.sharding import Mesh
from jax.sharding import PartitionSpec as P

HIGHEST = lax.Precision.HIGHEST
BLOCK = 32
CHUNKS = 2
VMEM_LIMIT = 24 * 2**20
VMEM_MOST = 64 * 2**20 - 440 * 2**10
VMEM = pl.BlockSpec(memory_space=pltpu.VMEM)
HBM = pl.BlockSpec(memory_space=pltpu.HBM)


def mm(a, b, on_a, on_b):
    return lax.dot_general(
        a,
        b,
        (((on_a,), (on_b,)), ((), ())),
        precision=HIGHEST,
        preferred_element_type=jnp.float32,
    )


def mm16(a, b):
    return jnp.dot(a, b, preferred_element_type=jnp.float32)


def three_parts(x):
    first = x.astype(jnp.bfloat16)
    rest = x - first.astype(jnp.float32)
    second = rest.astype(jnp.bfloat16)
    third = (rest - second.astype(jnp.float32)).astype(jnp.bfloat16)
    return first, second, third


def mm_wide(a, b):
    a, b = three_parts(a), three_parts(b)
    wide_a = jnp.concatenate([a[i] for i in (0, 0, 1, 0, 2, 1)], axis=1)
    wide_b = jnp.concatenate([b[i] for i in (0, 1, 0, 2, 0, 1)], axis=1)
    return lax.dot_general(
        wide_a, wide_b, (((1,), (1,)), ((), ())), preferred_element_type=jnp.float32
    )


def add_parts(x, axis):
    n = x.shape[axis] // 3
    a, b, c = (lax.slice_in_dim(x, i * n, (i + 1) * n, axis=axis) for i in range(3))
    return a + (b + c)


def diagonal(gram, axis):
    n = gram.shape[0]
    row = lax.broadcasted_iota(jnp.int32, (n, n), 0)
    lane = lax.broadcasted_iota(jnp.int32, (n, n), 1)
    return jnp.sum(jnp.where(row == lane, gram, 0.0), axis=axis, keepdims=True)


def small_inverse(block, width):
    n = block.shape[0]
    row = lax.broadcasted_iota(jnp.int32, (n, width), 0)
    lane = lax.broadcasted_iota(jnp.int32, (n, width), 1)
    inv = jnp.where(row == lane, 1.0, 0.0)
    cols = [jnp.broadcast_to(block[:, k : k + 1], (n, width)) for k in range(n)]
    for k in range(n):
        scale = lax.rsqrt(cols[k][k : k + 1, :])
        lower = cols[k] * scale
        pivot = inv[k : k + 1, :] * scale
        inv = jnp.where(
            row > k,
            inv - lower * pivot,
            jnp.where(row == k, jnp.broadcast_to(pivot, (n, width)), inv),
        )
        for j in range(k + 1, n):
            low = (j // 8) * 8
            new = cols[j][low:, :] - lower[low:, :] * lower[j : j + 1, :]
            cols[j] = new if low == 0 else jnp.concatenate([cols[j][:low, :], new], axis=0)
    return inv


def lower_inverse(gram):
    n = gram.shape[0]
    row = lax.broadcasted_iota(jnp.int32, (n, n), 0)
    lane = lax.broadcasted_iota(jnp.int32, (n, n), 1)
    left, right = gram, jnp.where(row == lane, 1.0, 0.0)
    out = []
    for start in range(0, n, BLOCK):
        small = small_inverse(left[:BLOCK, start : start + BLOCK], n)[:, :BLOCK]
        new_right = mm(small, right[:BLOCK, :], 1, 0)
        out.append(new_right)
        if start + BLOCK < n:
            new_left = mm(small, left[:BLOCK, :], 1, 0)
            below = new_left[:, start + BLOCK :]
            left = left[BLOCK:, :] - mm(below, new_left, 0, 0)
            right = right[BLOCK:, :] - mm(below, new_right, 0, 0)
    return jnp.concatenate(out, axis=0)


def left_product(grad, error, q_mat, scale):
    parts = jnp.concatenate(three_parts(q_mat), axis=1)
    return add_parts(mm16(grad, parts) + mm16(error, parts), 1) * scale


def first_left_kernel(scale, grad, error, q_mat, out, held, q_held, sems, q_sem):
    copies = [pltpu.make_async_copy(q_mat, q_held, q_sem)]
    for k, source in enumerate((grad, error)):
        copies.append(pltpu.make_async_copy(source.at[0], held.at[k], sems.at[k]))
    for copy in copies:
        copy.start()
    copies[0].wait()
    parts = jnp.concatenate(three_parts(q_held[...]), axis=1)
    copies[1].wait()
    product = mm16(held[0], parts)
    copies[2].wait()
    out[...] = add_parts(product + mm16(held[1], parts), 1) * scale


def next_left_kernel(scale, grad, error, both, out):
    cols = grad.shape[2]
    both = both[...].reshape(-1, both.shape[2])
    q_mat = both[:cols] * lax.rsqrt(diagonal(both[cols:], 0))
    out[...] = left_product(grad[0], error[0], q_mat, scale)


def right_kernel(scale, grad, error, p_mat, out):
    p_mat = p_mat[...].reshape(-1, p_mat.shape[2])
    p_t = p_mat.T
    parts = jnp.concatenate(three_parts(p_t), axis=0)
    term = add_parts(mm16(parts, grad[0]) + mm16(parts, error[0]), 0).T
    gram = mm(p_t, p_mat, 1, 0)
    both = jnp.concatenate([term, gram], axis=0) * scale
    out[...] = both.reshape(out.shape)


def sum_kernel(pieces, out):
    out[...] = jnp.broadcast_to(jnp.sum(pieces[...], axis=0)[None], out.shape)


def sum_scale_kernel(pieces, inverse, out):
    piece = mm(jnp.sum(pieces[...], axis=0), inverse[...], 1, 1)
    out[...] = jnp.broadcast_to(piece[None], out.shape)


def inverse_kernel(both, out):
    n = out.shape[0]
    gram = both[...].reshape(-1, n)[-n:]
    by_row = lax.rsqrt(diagonal(gram, 1))
    by_lane = lax.rsqrt(diagonal(gram, 0))
    out[...] = lower_inverse(gram * by_row * by_lane)


def core_sum_kernel(partials, out):
    out[...] = (partials[0] + partials[1]).reshape(out.shape)


def last_kernel(grad, error, p_mat, both, new_error, q_factor, held, q_held, sems, q_sem):
    cols = grad.shape[2]
    both = both[...].reshape(-1, both.shape[2])
    inverse = lower_inverse(both[cols:])
    q_mat = mm_wide(both[:cols], inverse)
    q_held[...] = q_mat
    copies = [pltpu.make_async_copy(q_held, q_factor, q_sem)]
    copies[0].start()
    p_hat = mm_wide(p_mat[...].reshape(-1, p_mat.shape[2]), inverse)
    rows = held.shape[1] // CHUNKS
    for i in range(CHUNKS):
        part = pl.ds(i * rows, rows)
        comp = grad[0, part, :].astype(jnp.float32) + error[0, part, :].astype(jnp.float32)
        approx = mm_wide(p_hat[i * rows : (i + 1) * rows], q_mat)
        held[0, part, :] = (comp - approx).astype(jnp.bfloat16)
        chunk = new_error.at[0, part, :]
        copies.append(pltpu.make_async_copy(held.at[0, part, :], chunk, sems.at[i]))
        copies[-1].start()
    for copy in copies:
        copy.wait()


def call(kernel, shapes, *operands, flops=10**8, **more):
    n_bytes = sum(x.size * x.dtype.itemsize for x in operands)
    n_bytes += sum(s.size * s.dtype.itemsize for s in jax.tree.leaves(shapes))
    return pl.pallas_call(
        kernel,
        out_shape=shapes,
        in_specs=more.pop("in_specs", [VMEM] * len(operands)),
        out_specs=more.pop("out_specs", VMEM),
        compiler_params=pltpu.CompilerParams(
            vmem_limit_bytes=more.pop("vmem_limit_bytes", VMEM_LIMIT)
        ),
        cost_estimate=pl.CostEstimate(flops=flops, bytes_accessed=n_bytes, transcendentals=0),
        **more,
    )(*operands)


def f32(*shape):
    return jax.ShapeDtypeStruct(shape, jnp.float32)


def exchange(x, axes):
    return lax.all_to_all(x, axes, 0, 0, tiled=True)


def shards(grad, error, q_init):
    rows, cols = grad.shape[1:]
    rank = q_init.shape[1]
    scale = 1.0 / lax.axis_size("dp")
    left_axes, right_axes = ("dp", "y"), ("dp", "row")
    n_left, n_right = lax.axis_size(left_axes), lax.axis_size(right_axes)
    left_shape = f32(n_left, rows // n_left, rank)
    right_shape = f32(n_right, (cols + rank) // n_right, rank)

    def left_pieces(partial):
        chip = call(core_sum_kernel, left_shape, lax.all_gather(partial, "core"))
        return exchange(chip, left_axes)

    def right_total(p_all):
        partial = call(functools.partial(right_kernel, scale), right_shape, grad, error, p_all)
        pieces = exchange(partial, right_axes)
        return exchange(call(sum_kernel, right_shape, pieces), right_axes)

    partial = call(
        functools.partial(first_left_kernel, scale),
        f32(rows, rank),
        grad,
        error,
        q_init,
        in_specs=[HBM] * 3,
        vmem_limit_bytes=VMEM_MOST,
        scratch_shapes=[
            pltpu.VMEM((2, rows, cols), jnp.bfloat16),
            pltpu.VMEM((cols, rank), jnp.float32),
            pltpu.SemaphoreType.DMA((2,)),
            pltpu.SemaphoreType.DMA,
        ],
    )
    pieces = left_pieces(partial)
    p_all = exchange(call(sum_kernel, left_shape, pieces), left_axes)
    both = right_total(p_all)
    partial = call(functools.partial(next_left_kernel, scale), f32(rows, rank), grad, error, both)
    inverse = call(inverse_kernel, f32(rank, rank), both, flops=4 * 10**9)
    pieces = left_pieces(partial)
    p_all = exchange(call(sum_scale_kernel, left_shape, pieces, inverse), left_axes)
    both = right_total(p_all)
    return call(
        last_kernel,
        (jax.ShapeDtypeStruct(grad.shape, jnp.bfloat16), f32(cols, rank)),
        grad,
        error,
        p_all,
        both,
        out_specs=(HBM, HBM),
        scratch_shapes=[
            pltpu.VMEM((1, rows, cols), jnp.bfloat16),
            pltpu.VMEM((cols, rank), jnp.float32),
            pltpu.SemaphoreType.DMA((CHUNKS,)),
            pltpu.SemaphoreType.DMA,
        ],
    )


def solution(mesh):
    size = mesh.devices.shape
    fine = Mesh(mesh.devices.reshape(*size[:2], size[2] // 2, 2), ("dp", "row", "y", "core"))
    block = P("dp", "row", ("y", "core"))
    right = P(("y", "core"), None)
    return jax.shard_map(
        shards, mesh=fine, in_specs=(block, block, right), out_specs=(block, right), check_vma=False
    )
```

```python
import functools

import jax
import jax.numpy as jnp
from jax import lax
from jax.experimental import pallas as pl
from jax.experimental.pallas import tpu as pltpu
from jax.sharding import Mesh
from jax.sharding import PartitionSpec as P

HIGHEST = lax.Precision.HIGHEST
BLOCK = 32
CHUNKS = 2
VMEM_LIMIT = 24 * 2**20
VMEM_MOST = 64 * 2**20 - 440 * 2**10
VMEM = pl.BlockSpec(memory_space=pltpu.VMEM)
HBM = pl.BlockSpec(memory_space=pltpu.HBM)


def mm(a, b, on_a, on_b):
    return lax.dot_general(
        a,
        b,
        (((on_a,), (on_b,)), ((), ())),
        precision=HIGHEST,
        preferred_element_type=jnp.float32,
    )


def mm16(a, b):
    return jnp.dot(a, b, preferred_element_type=jnp.float32)


def three_parts(x):
    first = x.astype(jnp.bfloat16)
    rest = x - first.astype(jnp.float32)
    second = rest.astype(jnp.bfloat16)
    third = (rest - second.astype(jnp.float32)).astype(jnp.bfloat16)
    return first, second, third


def mm_wide(a, b):
    a, b = three_parts(a), three_parts(b)
    wide_a = jnp.concatenate([a[i] for i in (0, 0, 1, 0, 2, 1)], axis=1)
    wide_b = jnp.concatenate([b[i] for i in (0, 1, 0, 2, 0, 1)], axis=1)
    return lax.dot_general(
        wide_a, wide_b, (((1,), (1,)), ((), ())), preferred_element_type=jnp.float32
    )


def add_parts(x, axis):
    n = x.shape[axis] // 3
    a, b, c = (lax.slice_in_dim(x, i * n, (i + 1) * n, axis=axis) for i in range(3))
    return a + (b + c)


def diagonal(gram, axis):
    n = gram.shape[0]
    row = lax.broadcasted_iota(jnp.int32, (n, n), 0)
    lane = lax.broadcasted_iota(jnp.int32, (n, n), 1)
    return jnp.sum(jnp.where(row == lane, gram, 0.0), axis=axis, keepdims=True)


def small_inverse(block, width):
    n = block.shape[0]
    row = lax.broadcasted_iota(jnp.int32, (n, width), 0)
    lane = lax.broadcasted_iota(jnp.int32, (n, width), 1)
    inv = jnp.where(row == lane, 1.0, 0.0)
    cols = [jnp.broadcast_to(block[:, k : k + 1], (n, width)) for k in range(n)]
    for k in range(n):
        scale = lax.rsqrt(cols[k][k : k + 1, :])
        lower = cols[k] * scale
        pivot = inv[k : k + 1, :] * scale
        inv = jnp.where(
            row > k,
            inv - lower * pivot,
            jnp.where(row == k, jnp.broadcast_to(pivot, (n, width)), inv),
        )
        for j in range(k + 1, n):
            low = (j // 8) * 8
            new = cols[j][low:, :] - lower[low:, :] * lower[j : j + 1, :]
            cols[j] = new if low == 0 else jnp.concatenate([cols[j][:low, :], new], axis=0)
    return inv


def lower_inverse(gram):
    n = gram.shape[0]
    row = lax.broadcasted_iota(jnp.int32, (n, n), 0)
    lane = lax.broadcasted_iota(jnp.int32, (n, n), 1)
    left, right = gram, jnp.where(row == lane, 1.0, 0.0)
    out = []
    for start in range(0, n, BLOCK):
        small = small_inverse(left[:BLOCK, start : start + BLOCK], n)[:, :BLOCK]
        new_right = mm(small, right[:BLOCK, :], 1, 0)
        out.append(new_right)
        if start + BLOCK < n:
            new_left = mm(small, left[:BLOCK, :], 1, 0)
            below = new_left[:, start + BLOCK :]
            left = left[BLOCK:, :] - mm(below, new_left, 0, 0)
            right = right[BLOCK:, :] - mm(below, new_right, 0, 0)
    return jnp.concatenate(out, axis=0)


def left_product(grad, error, q_mat, scale):
    parts = jnp.concatenate(three_parts(q_mat), axis=1)
    return add_parts(mm16(grad, parts) + mm16(error, parts), 1) * scale


def first_left_kernel(scale, grad, error, q_mat, out, held, q_held, sems, q_sem):
    copies = [pltpu.make_async_copy(q_mat, q_held, q_sem)]
    for k, source in enumerate((grad, error)):
        copies.append(pltpu.make_async_copy(source.at[0], held.at[k], sems.at[k]))
    for copy in copies:
        copy.start()
    copies[0].wait()
    parts = jnp.concatenate(three_parts(q_held[...]), axis=1)
    copies[1].wait()
    product = mm16(held[0], parts)
    copies[2].wait()
    out[...] = add_parts(product + mm16(held[1], parts), 1) * scale


def second_core_inverse(gram, out):
    second = lax.axis_index("core") == 1

    @pl.when(second)
    def _():
        out[...] = lower_inverse(gram)

    @pl.when(jnp.logical_not(second))
    def _():
        out[...] = jnp.zeros_like(out)


def next_left_kernel(scale, grad, error, both, out):
    rows, cols = grad.shape[1:]
    both = both[...].reshape(-1, both.shape[2])
    gram = both[cols:]
    by_lane = lax.rsqrt(diagonal(gram, 0))
    product = left_product(grad[0], error[0], both[:cols] * by_lane, scale)
    out[pl.ds(0, rows), :] = product
    by_row = lax.rsqrt(diagonal(gram, 1))
    second_core_inverse(gram * by_row * by_lane, out.at[pl.ds(rows, gram.shape[0]), :])


def right_kernel(scale, grad, error, p_mat, out):
    p_mat = p_mat[...].reshape(-1, p_mat.shape[2])
    p_t = p_mat.T
    parts = jnp.concatenate(three_parts(p_t), axis=0)
    term = add_parts(mm16(parts, grad[0]) + mm16(parts, error[0]), 0).T
    gram = mm(p_t, p_mat, 1, 0)
    both = jnp.concatenate([term, gram], axis=0) * scale
    out[...] = both.reshape(out.shape)


def sum_kernel(pieces, out):
    out[...] = jnp.broadcast_to(jnp.sum(pieces[...], axis=0)[None], out.shape)


def sum_scale_kernel(pieces, inverse, out):
    piece = mm(jnp.sum(pieces[...], axis=0), inverse[...], 1, 1)
    out[...] = jnp.broadcast_to(piece[None], out.shape)


def inverse_kernel(both, out):
    n = out.shape[0]
    second_core_inverse(both[...].reshape(-1, n)[-n:], out)


def core_sum_kernel(partials, out):
    out[...] = (partials[0] + partials[1]).reshape(out.shape)


def core_sum_inverse_kernel(partials, out, inverse):
    rows = partials.shape[1] - inverse.shape[0]
    out[...] = (partials[0, :rows] + partials[1, :rows]).reshape(out.shape)
    inverse[...] = partials[1, rows:]


def last_kernel(grad, error, p_mat, both, inverses, new_error, q_factor, held, q_held, sems, q_sem):
    cols = grad.shape[2]
    both = both[...].reshape(-1, both.shape[2])
    inverse = inverses[1]
    q_mat = mm_wide(both[:cols], inverse)
    q_held[...] = q_mat
    copies = [pltpu.make_async_copy(q_held, q_factor, q_sem)]
    copies[0].start()
    p_hat = mm_wide(p_mat[...].reshape(-1, p_mat.shape[2]), inverse)
    rows = held.shape[1] // CHUNKS
    for i in range(CHUNKS):
        part = pl.ds(i * rows, rows)
        comp = grad[0, part, :].astype(jnp.float32) + error[0, part, :].astype(jnp.float32)
        approx = mm_wide(p_hat[i * rows : (i + 1) * rows], q_mat)
        held[0, part, :] = (comp - approx).astype(jnp.bfloat16)
        chunk = new_error.at[0, part, :]
        copies.append(pltpu.make_async_copy(held.at[0, part, :], chunk, sems.at[i]))
        copies[-1].start()
    for copy in copies:
        copy.wait()


def call(kernel, shapes, *operands, flops=10**8, **more):
    n_bytes = sum(x.size * x.dtype.itemsize for x in operands)
    n_bytes += sum(s.size * s.dtype.itemsize for s in jax.tree.leaves(shapes))
    return pl.pallas_call(
        kernel,
        out_shape=shapes,
        in_specs=more.pop("in_specs", [VMEM] * len(operands)),
        out_specs=more.pop("out_specs", VMEM),
        compiler_params=pltpu.CompilerParams(
            vmem_limit_bytes=more.pop("vmem_limit_bytes", VMEM_LIMIT)
        ),
        cost_estimate=pl.CostEstimate(flops=flops, bytes_accessed=n_bytes, transcendentals=0),
        **more,
    )(*operands)


def f32(*shape):
    return jax.ShapeDtypeStruct(shape, jnp.float32)


def exchange(x, axes):
    return lax.all_to_all(x, axes, 0, 0, tiled=True)


def shards(grad, error, q_init):
    rows, cols = grad.shape[1:]
    rank = q_init.shape[1]
    scale = 1.0 / lax.axis_size("dp")
    left_axes, right_axes = ("dp", "y"), ("dp", "row")
    n_left, n_right = lax.axis_size(left_axes), lax.axis_size(right_axes)
    left_shape = f32(n_left, rows // n_left, rank)
    right_shape = f32(n_right, (cols + rank) // n_right, rank)

    def right_total(p_all):
        partial = call(functools.partial(right_kernel, scale), right_shape, grad, error, p_all)
        pieces = exchange(partial, right_axes)
        return exchange(call(sum_kernel, right_shape, pieces), right_axes)

    partial = call(
        functools.partial(first_left_kernel, scale),
        f32(rows, rank),
        grad,
        error,
        q_init,
        in_specs=[HBM] * 3,
        vmem_limit_bytes=VMEM_MOST,
        scratch_shapes=[
            pltpu.VMEM((2, rows, cols), jnp.bfloat16),
            pltpu.VMEM((cols, rank), jnp.float32),
            pltpu.SemaphoreType.DMA((2,)),
            pltpu.SemaphoreType.DMA,
        ],
    )
    chip = call(core_sum_kernel, left_shape, lax.all_gather(partial, "core"))
    pieces = exchange(chip, left_axes)
    p_all = exchange(call(sum_kernel, left_shape, pieces), left_axes)
    both = right_total(p_all)
    partial = call(
        functools.partial(next_left_kernel, scale), f32(rows + rank, rank), grad, error, both
    )
    chip, inverse = call(
        core_sum_inverse_kernel,
        (left_shape, f32(rank, rank)),
        lax.all_gather(partial, "core"),
        out_specs=(VMEM, VMEM),
    )
    pieces = exchange(chip, left_axes)
    p_all = exchange(call(sum_scale_kernel, left_shape, pieces, inverse), left_axes)
    both = right_total(p_all)
    inverses = lax.all_gather(call(inverse_kernel, f32(rank, rank), both), "core")
    return call(
        last_kernel,
        (jax.ShapeDtypeStruct(grad.shape, jnp.bfloat16), f32(cols, rank)),
        grad,
        error,
        p_all,
        both,
        inverses,
        out_specs=(HBM, HBM),
        scratch_shapes=[
            pltpu.VMEM((1, rows, cols), jnp.bfloat16),
            pltpu.VMEM((cols, rank), jnp.float32),
            pltpu.SemaphoreType.DMA((CHUNKS,)),
            pltpu.SemaphoreType.DMA,
        ],
    )


def solution(mesh):
    size = mesh.devices.shape
    fine = Mesh(mesh.devices.reshape(*size[:2], size[2] // 2, 2), ("dp", "row", "y", "core"))
    block = P("dp", "row", ("y", "core"))
    right = P(("y", "core"), None)
    return jax.shard_map(
        shards, mesh=fine, in_specs=(block, block, right), out_specs=(block, right), check_vma=False
    )
```

```python
import functools

import jax
import jax.numpy as jnp
from jax import lax
from jax.experimental import pallas as pl
from jax.experimental.pallas import tpu as pltpu
from jax.sharding import Mesh
from jax.sharding import PartitionSpec as P

HIGHEST = lax.Precision.HIGHEST
BLOCK = 32
CHUNKS = 2
VMEM_LIMIT = 24 * 2**20
VMEM_MOST = 64 * 2**20 - 440 * 2**10
VMEM = pl.BlockSpec(memory_space=pltpu.VMEM)
HBM = pl.BlockSpec(memory_space=pltpu.HBM)


def mm(a, b, on_a, on_b):
    return lax.dot_general(
        a,
        b,
        (((on_a,), (on_b,)), ((), ())),
        precision=HIGHEST,
        preferred_element_type=jnp.float32,
    )


def mm16(a, b):
    return jnp.dot(a, b, preferred_element_type=jnp.float32)


def three_parts(x):
    first = x.astype(jnp.bfloat16)
    rest = x - first.astype(jnp.float32)
    second = rest.astype(jnp.bfloat16)
    third = (rest - second.astype(jnp.float32)).astype(jnp.bfloat16)
    return first, second, third


def mm_wide(a, b):
    a, b = three_parts(a), three_parts(b)
    wide_a = jnp.concatenate([a[i] for i in (0, 0, 1, 0, 2, 1)], axis=1)
    wide_b = jnp.concatenate([b[i] for i in (0, 1, 0, 2, 0, 1)], axis=1)
    return lax.dot_general(
        wide_a, wide_b, (((1,), (1,)), ((), ())), preferred_element_type=jnp.float32
    )


def add_parts(x, axis):
    n = x.shape[axis] // 3
    a, b, c = (lax.slice_in_dim(x, i * n, (i + 1) * n, axis=axis) for i in range(3))
    return a + (b + c)


def diagonal(gram, axis):
    n = gram.shape[0]
    row = lax.broadcasted_iota(jnp.int32, (n, n), 0)
    lane = lax.broadcasted_iota(jnp.int32, (n, n), 1)
    return jnp.sum(jnp.where(row == lane, gram, 0.0), axis=axis, keepdims=True)


def small_inverse(block, width):
    n = block.shape[0]
    row = lax.broadcasted_iota(jnp.int32, (n, width), 0)
    lane = lax.broadcasted_iota(jnp.int32, (n, width), 1)
    inv = jnp.where(row == lane, 1.0, 0.0)
    cols = [jnp.broadcast_to(block[:, k : k + 1], (n, width)) for k in range(n)]
    for k in range(n):
        scale = lax.rsqrt(cols[k][k : k + 1, :])
        lower = cols[k] * scale
        pivot = inv[k : k + 1, :] * scale
        inv = jnp.where(
            row > k,
            inv - lower * pivot,
            jnp.where(row == k, jnp.broadcast_to(pivot, (n, width)), inv),
        )
        for j in range(k + 1, n):
            low = (j // 8) * 8
            new = cols[j][low:, :] - lower[low:, :] * lower[j : j + 1, :]
            cols[j] = new if low == 0 else jnp.concatenate([cols[j][:low, :], new], axis=0)
    return inv


def lower_inverse(gram):
    n = gram.shape[0]
    row = lax.broadcasted_iota(jnp.int32, (n, n), 0)
    lane = lax.broadcasted_iota(jnp.int32, (n, n), 1)
    left, right = gram, jnp.where(row == lane, 1.0, 0.0)
    out = []
    for start in range(0, n, BLOCK):
        small = small_inverse(left[:BLOCK, start : start + BLOCK], n)[:, :BLOCK]
        new_right = mm(small, right[:BLOCK, :], 1, 0)
        out.append(new_right)
        if start + BLOCK < n:
            new_left = mm(small, left[:BLOCK, :], 1, 0)
            below = new_left[:, start + BLOCK :]
            left = left[BLOCK:, :] - mm(below, new_left, 0, 0)
            right = right[BLOCK:, :] - mm(below, new_right, 0, 0)
    return jnp.concatenate(out, axis=0)


def left_product(grad, error, q_mat, scale):
    parts = jnp.concatenate(three_parts(q_mat), axis=1)
    return add_parts(mm16(grad, parts) + mm16(error, parts), 1) * scale


def first_left_kernel(scale, grad, error, q_mat, out, held, q_held, sems, q_sem):
    copies = [pltpu.make_async_copy(q_mat, q_held, q_sem)]
    for k, source in enumerate((grad, error)):
        copies.append(pltpu.make_async_copy(source.at[0], held.at[k], sems.at[k]))
    for copy in copies:
        copy.start()
    copies[0].wait()
    parts = jnp.concatenate(three_parts(q_held[...]), axis=1)
    copies[1].wait()
    product = mm16(held[0], parts)
    copies[2].wait()
    out[...] = add_parts(product + mm16(held[1], parts), 1) * scale


def next_left_kernel(scale, grad, error, both, out):
    cols = grad.shape[2]
    both = both[...].reshape(-1, both.shape[2])
    q_mat = both[:cols] * lax.rsqrt(diagonal(both[cols:], 0))
    out[...] = left_product(grad[0], error[0], q_mat, scale)


def right_kernel(scale, grad, error, p_mat, out):
    p_mat = p_mat[...].reshape(-1, p_mat.shape[2])
    p_t = p_mat.T
    parts = jnp.concatenate(three_parts(p_t), axis=0)
    term = add_parts(mm16(parts, grad[0]) + mm16(parts, error[0]), 0).T
    gram = mm(p_t, p_mat, 1, 0)
    both = jnp.concatenate([term, gram], axis=0) * scale
    out[...] = both.reshape(out.shape)


def sum_kernel(pieces, out):
    out[...] = jnp.broadcast_to(jnp.sum(pieces[...], axis=0)[None], out.shape)


def sum_scale_kernel(pieces, inverse, out):
    piece = mm(jnp.sum(pieces[...], axis=0), inverse[...], 1, 1)
    out[...] = jnp.broadcast_to(piece[None], out.shape)


def inverse_kernel(both, out):
    n = out.shape[0]
    gram = both[...].reshape(-1, n)[-n:]
    by_row = lax.rsqrt(diagonal(gram, 1))
    by_lane = lax.rsqrt(diagonal(gram, 0))
    out[...] = lower_inverse(gram * by_row * by_lane)


def core_half_kernel(partials, out):
    rows = out.shape[0]
    start = pl.multiple_of(lax.axis_index("core") * rows, rows)
    out[...] = partials[0, pl.ds(start, rows), :] + partials[1, pl.ds(start, rows), :]


def core_sum_kernel(partials, out):
    out[...] = (partials[0] + partials[1]).reshape(out.shape)


def last_kernel(grad, error, p_mat, both, new_error, q_factor, held, q_held, sems, q_sem):
    cols = grad.shape[2]
    both = both[...].reshape(-1, both.shape[2])
    inverse = lower_inverse(both[cols:])
    q_mat = mm_wide(both[:cols], inverse)
    q_held[...] = q_mat
    copies = [pltpu.make_async_copy(q_held, q_factor, q_sem)]
    copies[0].start()
    p_hat = mm_wide(p_mat[...].reshape(-1, p_mat.shape[2]), inverse)
    rows = held.shape[1] // CHUNKS
    for i in range(CHUNKS):
        part = pl.ds(i * rows, rows)
        comp = grad[0, part, :].astype(jnp.float32) + error[0, part, :].astype(jnp.float32)
        approx = mm_wide(p_hat[i * rows : (i + 1) * rows], q_mat)
        held[0, part, :] = (comp - approx).astype(jnp.bfloat16)
        chunk = new_error.at[0, part, :]
        copies.append(pltpu.make_async_copy(held.at[0, part, :], chunk, sems.at[i]))
        copies[-1].start()
    for copy in copies:
        copy.wait()


def call(kernel, shapes, *operands, flops=10**8, **more):
    n_bytes = sum(x.size * x.dtype.itemsize for x in operands)
    n_bytes += sum(s.size * s.dtype.itemsize for s in jax.tree.leaves(shapes))
    return pl.pallas_call(
        kernel,
        out_shape=shapes,
        in_specs=more.pop("in_specs", [VMEM] * len(operands)),
        out_specs=more.pop("out_specs", VMEM),
        compiler_params=pltpu.CompilerParams(
            vmem_limit_bytes=more.pop("vmem_limit_bytes", VMEM_LIMIT)
        ),
        cost_estimate=pl.CostEstimate(flops=flops, bytes_accessed=n_bytes, transcendentals=0),
        **more,
    )(*operands)


def f32(*shape):
    return jax.ShapeDtypeStruct(shape, jnp.float32)


def exchange(x, axes):
    return lax.all_to_all(x, axes, 0, 0, tiled=True)


def shards(grad, error, q_init):
    rows, cols = grad.shape[1:]
    rank = q_init.shape[1]
    scale = 1.0 / lax.axis_size("dp")
    left_axes, right_axes = ("dp", "y"), ("dp", "row")
    n_left, n_right = lax.axis_size(left_axes), lax.axis_size(right_axes)
    left_shape = f32(n_left, rows // n_left, rank)
    right_shape = f32(n_right, (cols + rank) // n_right, rank)

    def right_total(p_all):
        partial = call(functools.partial(right_kernel, scale), right_shape, grad, error, p_all)
        pieces = exchange(partial, right_axes)
        return exchange(call(sum_kernel, right_shape, pieces), right_axes)

    partial = call(
        functools.partial(first_left_kernel, scale),
        f32(rows, rank),
        grad,
        error,
        q_init,
        in_specs=[HBM] * 3,
        vmem_limit_bytes=VMEM_MOST,
        scratch_shapes=[
            pltpu.VMEM((2, rows, cols), jnp.bfloat16),
            pltpu.VMEM((cols, rank), jnp.float32),
            pltpu.SemaphoreType.DMA((2,)),
            pltpu.SemaphoreType.DMA,
        ],
    )
    half = rows // lax.axis_size("core")
    half_shape = f32(n_left, half // n_left, rank)
    mine = call(core_half_kernel, f32(half, rank), lax.all_gather(partial, "core"))
    pieces = exchange(mine.reshape(half_shape.shape), left_axes)
    mine = exchange(call(sum_kernel, half_shape, pieces), left_axes).reshape(half, rank)
    p_all = lax.all_gather(mine, "core", tiled=True).reshape(left_shape.shape)
    both = right_total(p_all)
    partial = call(functools.partial(next_left_kernel, scale), f32(rows, rank), grad, error, both)
    inverse = call(inverse_kernel, f32(rank, rank), both, flops=4 * 10**9)
    chip = call(core_sum_kernel, left_shape, lax.all_gather(partial, "core"))
    pieces = exchange(chip, left_axes)
    p_all = exchange(call(sum_scale_kernel, left_shape, pieces, inverse), left_axes)
    both = right_total(p_all)
    return call(
        last_kernel,
        (jax.ShapeDtypeStruct(grad.shape, jnp.bfloat16), f32(cols, rank)),
        grad,
        error,
        p_all,
        both,
        out_specs=(HBM, HBM),
        scratch_shapes=[
            pltpu.VMEM((1, rows, cols), jnp.bfloat16),
            pltpu.VMEM((cols, rank), jnp.float32),
            pltpu.SemaphoreType.DMA((CHUNKS,)),
            pltpu.SemaphoreType.DMA,
        ],
    )


def solution(mesh):
    size = mesh.devices.shape
    fine = Mesh(mesh.devices.reshape(*size[:2], size[2] // 2, 2), ("dp", "row", "y", "core"))
    block = P("dp", "row", ("y", "core"))
    right = P(("y", "core"), None)
    return jax.shard_map(
        shards, mesh=fine, in_specs=(block, block, right), out_specs=(block, right), check_vma=False
    )
```
